256 devices in a mesh: dp: 16 (over x_hi, z), ctx: 16 (over x_lo, y, core).
Axes of the slice: x: 4 (x_hi: 2, x_lo: 2; x = x_hi * 2 + x_lo), y: 4, z: 8, core: 2. Of those that a mesh axis runs over, the one named last changes fastest.
Arguments:
- queries: bfloat16 [16, 3584, 1024], P('dp', 'ctx'), may hold values from -5 to 5
- keys: bfloat16 [16, 3584, 128], P('dp', 'ctx'), may hold values from -5 to 5
- values: bfloat16 [16, 3584, 128], P('dp', 'ctx'), may hold values from -6 to 6
- out_grad: bfloat16 [16, 3584, 1024], P('dp', 'ctx'), may hold values from -6 to 6
- segments: int32 [16, 3584], P('dp', 'ctx'), may hold values from 0 to 2, never falling along the last dimension, each value on 1 to 2688 neighbouring positions
- features: bfloat16 [16, 3584, 8192], P('dp', 'ctx'), may hold values from -6 to 6
- projector: bfloat16 [8192, 512], P('dp'), may hold values from -0.25 to 0.25
- first_moment: float32 [512, 256], P(('dp', 'ctx')), may hold values from -10 to 10, as said below
- second_moment: float32 [512, 256], P(('dp', 'ctx')), may hold values from 0.01 to 100
- adam_step: int32 [1], replicated, may hold values from 10 to 1000
Outputs:
- query_grad: bfloat16 [16, 3584, 1024], P('dp', 'ctx')
- update: float32 [8192, 256], P(('dp', 'ctx'))
- first_new: float32 [512, 256], P(('dp', 'ctx'))
- second_new: float32 [512, 256], P(('dp', 'ctx'))
The draws below stay inside these ranges and needn't reach their ends.
Inputs may be any that keep to these rules, and one draw needn't show every extreme that they name: `segments`: segment numbers never fall along a sequence; a document holds 1 to 2688 tokens and one holds exactly that many. `first_moment`: each entry's magnitude is at most the square root of the same entry of second_moment.
All inputs are finite; a program needn't handle non-finite values.
Results may differ from the reference program's by a relative error of at most 0.0044.
The reference program's roundings to bfloat16 on the way (of `dscore`, `probs_low` and `kv_grad`) count: a program that leaves them out, or rounds other values in their place, can miss the bound.
Values may be sent and summed in bfloat16 or wider, within the bound.
No kernel may reach another device: no remote copies, remote signals or barrier semaphores. Data moves between devices by JAX's collectives and lax.ppermute only.
A program may use at most 64 MiB of HBM per device.

```python
import math
import jax
import jax.numpy as jnp
import numpy as np
from jax import lax

D = 8192
HEADS = 8
HD = 128
RANK = 512
QW = 1024
KVW = 256
SEQ = 3584
BATCH = 16


SHARP = 5.0


def moment_pair(key):
    base = jax.random.fold_in(key, 5)
    spread = jax.random.uniform(jax.random.fold_in(base, 1), (RANK, KVW), jnp.float32, math.log(0.01), math.log(100.0))
    second_values = jnp.exp(spread)
    ratio = jax.random.uniform(jax.random.fold_in(base, 2), (RANK, KVW), jnp.float32, -1.0, 1.0)
    return (ratio * jnp.sqrt(second_values), second_values)


def draw_queries(key, part):
    values_now = jnp.clip(jax.random.normal(jax.random.fold_in(key, 11), (BATCH, SEQ, QW), jnp.float32), -SHARP, SHARP)
    return values_now.astype(jnp.bfloat16)


def draw_keys(key, part):
    values_now = jnp.clip(jax.random.normal(jax.random.fold_in(key, 13), (BATCH, SEQ, HD), jnp.float32), -SHARP, SHARP)
    return values_now.astype(jnp.bfloat16)


def draw_first_moment(key, part):
    first_values, second_values = moment_pair(key)
    return first_values


def draw_second_moment(key, part):
    first_values, second_values = moment_pair(key)
    return second_values


def shard_levels(stream_key, extent, pieces, smallest, top_value):
    gain, own = 1.0, jax.random.fold_in(stream_key, 6)
    for position, blocks in pieces:
        heights = jnp.exp(jax.random.uniform(jax.random.fold_in(own, position), (blocks,), jnp.float32, smallest / len(pieces), top_value / len(pieces)))
        gain = gain * jnp.repeat(heights, extent[position] // blocks).reshape([-1 if axis == position else 1 for axis in range(len(extent))])
    return gain


def profile(number_of, total, most, lean):
    weights = [(1 << 20) // math.isqrt(standing ** lean) + 1 for standing in range(2, number_of + 1)]
    rest, counts = total - most - (number_of - 1), [1] * (number_of - 1)
    while rest > 0:
        candidates = [i for i in range(number_of - 1) if counts[i] < most]
        whole, left = sum([weights[i] for i in candidates]), rest
        for i in candidates:
            extra = min(most - counts[i], max(1, left * weights[i] // whole), rest)
            counts[i] = counts[i] + extra
            rest = rest - extra
    return np.array([most] + counts)


def ragged(stream_key, number_of, total, reach, slope):
    if number_of == 2:
        one = jax.random.randint(stream_key, (), max(1, total - reach), min(reach, total - 1) + 1)
        return jnp.stack([one, total - one])
    lengths = jnp.asarray(profile(number_of, total, reach, slope), jnp.int32)
    pairs = (number_of - 1) // 2
    source_of, sink = lengths[1:1 + 2 * pairs:2], lengths[2:2 + 2 * pairs:2]
    margin = jnp.minimum(source_of - 1, reach - sink)
    shifted = jax.random.randint(jax.random.fold_in(stream_key, 1), (pairs,), 0, 1 << 20) % (margin + 1)
    lengths = lengths.at[1:1 + 2 * pairs:2].set(source_of - shifted).at[2:2 + 2 * pairs:2].set(sink + shifted)
    return lengths[jax.random.permutation(jax.random.fold_in(stream_key, 2), number_of)]


def bell_draw(stream_key, shape, deviation, most, pieces=(), held_as=jnp.bfloat16):
    entries = jax.random.normal(stream_key, shape, jnp.float32) * deviation
    if len(pieces) > 0:
        entries = shard_levels(stream_key, shape, pieces, -0.22, 0.18) * entries
    return jnp.clip(entries, min=-most, max=most).astype(held_as)


def setup_inputs(seed: int = 0) -> dict:
    key_of = jax.random.split(jax.random.key(seed), 11)
    queries = draw_queries(jax.random.fold_in(key_of[10], 71), 0)
    keys = draw_keys(jax.random.fold_in(key_of[10], 71), 0)
    values = bell_draw(key_of[2], (BATCH, SEQ, HD), 1.0, 6.0, ((0, 16), (1, 16)))
    out_grad = bell_draw(key_of[3], (BATCH, SEQ, QW), 1.0, 6.0, ((0, 16), (1, 16)))
    segments = jax.vmap(lambda own: jnp.searchsorted(jnp.cumsum(ragged(own, 3, SEQ, 3 * SEQ // 4, 0)), jnp.arange(SEQ), side="right"))(jax.random.split(key_of[4], BATCH)).reshape((BATCH, SEQ)).astype(jnp.int32)
    features = bell_draw(key_of[5], (BATCH, SEQ, D), 1.0, 6.0, ((0, 16), (1, 16)))
    projector = bell_draw(key_of[6], (D, RANK), RANK ** -0.5, 0.25, ((0, 16),))
    first_moment = draw_first_moment(jax.random.fold_in(key_of[10], 71), 0)
    second_moment = draw_second_moment(jax.random.fold_in(key_of[10], 71), 0)
    adam_step = jax.random.randint(key_of[9], (1,), 10, 1001).astype(jnp.int32)
    return dict(queries=queries, keys=keys, values=values, out_grad=out_grad, segments=segments, features=features, projector=projector, first_moment=first_moment, second_moment=second_moment, adam_step=adam_step)


BETA_ONE = 0.9
BETA_TWO = 0.999
EPSILON = 1e-08

def group_backward(queries_g, keys_g, values_g, grads_g, segments_g):
    seq_len = queries_g.shape[0]
    scale = 1.0 / math.sqrt(HD)
    positions = jnp.arange(seq_len, dtype=jnp.int32)
    allowed = (positions[None, :] <= positions[:, None]) & (segments_g[None, :] == segments_g[:, None])
    query_heads = jnp.transpose(queries_g.reshape(seq_len, HEADS, HD), (1, 0, 2))
    grad_heads = jnp.transpose(grads_g.reshape(seq_len, HEADS, HD), (1, 0, 2))

    def one_head(pair):
        query_one, grad_one = pair
        scores = jnp.dot(query_one, keys_g.T, preferred_element_type=jnp.float32) * scale
        masked = jnp.where(allowed, scores, -jnp.inf)
        row_top = lax.optimization_barrier(jnp.max(masked, axis=1, keepdims=True))
        log_total = row_top + jnp.log(lax.optimization_barrier(jnp.sum(jnp.exp(masked - row_top), axis=1, keepdims=True)))
        probs = jnp.where(allowed, jnp.exp(masked - log_total), 0.0)
        dprob = jnp.dot(grad_one, values_g.T, preferred_element_type=jnp.float32)
        delta = lax.optimization_barrier(jnp.sum(probs * dprob, axis=1, keepdims=True))
        dscore = (probs * (dprob - delta)).astype(jnp.bfloat16)
        probs_low = probs.astype(jnp.bfloat16)
        query_part = (jnp.dot(dscore, keys_g, preferred_element_type=jnp.float32) * scale).astype(jnp.bfloat16)
        key_part = jnp.dot(dscore.T, query_one, preferred_element_type=jnp.float32) * scale
        value_part = jnp.dot(probs_low.T, grad_one, preferred_element_type=jnp.float32)
        return (query_part, key_part, value_part)
    query_part, key_part, value_part = lax.map(one_head, (query_heads, grad_heads))
    query_grad = jnp.transpose(query_part, (1, 0, 2)).reshape(seq_len, HEADS * HD)
    kv_grad = jnp.concatenate([lax.optimization_barrier(jnp.sum(key_part, axis=0)), lax.optimization_barrier(jnp.sum(value_part, axis=0))], axis=1).astype(jnp.bfloat16)
    return (query_grad, kv_grad)

def reference(queries, keys, values, out_grad, segments, features, projector, first_moment, second_moment, adam_step):

    def per_group(grad_total, items):
        queries_g, keys_g, values_g, grads_g, segments_g, features_g = items
        query_grad, kv_grad = group_backward(queries_g, keys_g, values_g, grads_g, segments_g)
        grad_total = grad_total + jnp.dot(features_g.T, kv_grad, preferred_element_type=jnp.float32)
        return (grad_total, query_grad)
    weight_grad, query_grad = lax.scan(per_group, jnp.zeros((D, 2 * HD), jnp.float32), (queries, keys, values, out_grad, segments, features))
    projector_wide = projector.astype(jnp.float32)
    projected = jnp.dot(projector_wide.T, weight_grad, precision=lax.Precision.HIGHEST)
    first_new = BETA_ONE * first_moment + (1.0 - BETA_ONE) * projected
    second_new = BETA_TWO * second_moment + (1.0 - BETA_TWO) * projected * projected
    step_count = adam_step[0].astype(jnp.float32)
    bias_first = 1.0 - jnp.power(jnp.float32(BETA_ONE), step_count)
    bias_second = 1.0 - jnp.power(jnp.float32(BETA_TWO), step_count)
    direction = first_new / bias_first / (jnp.sqrt(second_new / bias_second) + EPSILON)
    update = jnp.dot(projector_wide, direction, precision=lax.Precision.HIGHEST)
    return (query_grad, update, first_new, second_new)
```

```python
import functools
import math

import jax
import jax.numpy as jnp
from jax import lax
from jax.experimental import pallas as pl
from jax.experimental.pallas import tpu as pltpu
from jax.sharding import PartitionSpec as P

HEADS = 8
BETA_ONE = 0.9
BETA_TWO = 0.999
EPSILON = 1e-08
LONGEST = 2688
PAD = 16
CHUNK = 256
BF = jnp.bfloat16
F32 = jnp.float32

CORE_PAIRS = [(i, i ^ 1) for i in range(16)]
SAME_CORE = [list(range(0, 16, 2)), list(range(1, 16, 2))]
FAR_PAIRS = [(i, i ^ 8) for i in range(16)]
Z_RINGS = [list(range(8)), list(range(8, 16))]
SAME_CORE_ALL = [list(range(0, 256, 2)), list(range(1, 256, 2))]


def attention_kernel(
    place_ref,
    seg_ref,
    own_kv,
    other_kv,
    q_ref,
    do_ref,
    dq_ref,
    own_out,
    other_out,
    qs,
    dos,
    e_scr,
    dp_scr,
    tops,
    top,
    total,
    weighted,
    start_scr,
    p_scr,
    ds_scr,
    dq_acc,
    dq_rows,
):
    rows = q_ref.shape[0]
    hd = q_ref.shape[1] // HEADS
    cols = rows * HEADS
    me = place_ref[0]
    core = lax.rem(me, 2)
    scale = 1.0 / math.sqrt(hd)
    scale_two = scale * math.log2(math.e)
    chunks = cols // CHUNK
    for h in range(HEADS):
        qs[h * rows : (h + 1) * rows, :] = q_ref[:, h * hd : (h + 1) * hd]
        dos[h * rows : (h + 1) * rows, :] = do_ref[:, h * hd : (h + 1) * hd]
    own_out[...] = jnp.zeros_like(own_out)
    other_out[...] = jnp.zeros_like(other_out)
    counts = jnp.zeros((PAD, 2 * hd), F32)
    for chip in range(own_kv.shape[0]):
        counts = counts + own_kv[chip, rows : rows + PAD, :].astype(F32)
        counts = counts + other_kv[chip, rows : rows + PAD, :].astype(F32)
    first = counts[0:1, :]
    second = first + counts[8:9, :]
    low = None
    high = None
    for c in range(chunks):
        at = slice(c * CHUNK, (c + 1) * CHUNK)
        seg = seg_ref[:, at]
        start = jnp.where(seg == 0, 0.0, jnp.where(seg == 1, first, second))
        start_scr[:, at] = start
        low = start if low is None else jnp.minimum(low, start)
        high = start if high is None else jnp.maximum(high, start)
    low_block = lax.div(jnp.min(low).astype(jnp.int32), rows)
    high_key = jnp.max(high).astype(jnp.int32)
    top[...] = jnp.full_like(top, -1e29)
    total[...] = jnp.zeros_like(total)
    weighted[...] = jnp.zeros_like(weighted)
    dq_acc[...] = jnp.zeros_like(dq_acc)

    def kv_block(block, lanes):
        chip = lax.div(block, 2)
        mine = lax.rem(block, 2) == core
        return jnp.where(mine, own_kv[chip, 0:rows, lanes], other_kv[chip, 0:rows, lanes])

    def first_pass(block, masked):
        slot = block - low_block
        key = kv_block(block, slice(0, hd))
        value = kv_block(block, slice(hd, 2 * hd))
        for c in range(chunks):
            at = slice(c * CHUNK, (c + 1) * CHUNK)
            s = lax.dot_general(
                key, qs[at, :], (((1,), (1,)), ((), ())), preferred_element_type=F32
            )
            dp = lax.dot_general(
                value, dos[at, :], (((1,), (1,)), ((), ())), preferred_element_type=F32
            )
            s = s * scale_two
            if masked:
                row = lax.broadcasted_iota(jnp.int32, (rows, CHUNK), 0) + block * rows
                column = lax.broadcasted_iota(jnp.int32, (1, CHUNK), 1) + c * CHUNK
                pos = lax.rem(column, rows) + me * rows
                start = start_scr[:, at].astype(jnp.int32)
                s = jnp.where((row <= pos) & (row >= start), s, -1e30)
            old = top[:, at]
            new = jnp.maximum(old, jnp.max(s, axis=0, keepdims=True))
            e = jnp.exp2(s - new)
            factor = jnp.exp2(old - new)
            top[:, at] = new
            tops[pl.ds(slot, 1), at] = new
            total[:, at] = total[:, at] * factor + jnp.sum(e, axis=0, keepdims=True)
            weighted[:, at] = weighted[:, at] * factor + jnp.sum(e * dp, axis=0, keepdims=True)
            e_scr[slot, :, at] = e
            dp_scr[slot, :, at] = dp

    @pl.loop(low_block, me + 1)
    def _(block):
        edge = (block == me) | (block * rows < high_key)

        @pl.when(edge)
        def _():
            first_pass(block, True)

        @pl.when(jnp.logical_not(edge))
        def _():
            first_pass(block, False)

    inverse = 1.0 / total[...]
    total[...] = inverse
    weighted[...] = weighted[...] * inverse

    @pl.loop(low_block, me + 1)
    def _(block):
        slot = block - low_block
        for c in range(chunks):
            at = slice(c * CHUNK, (c + 1) * CHUNK)
            factor = jnp.exp2(tops[pl.ds(slot, 1), at] - top[:, at]) * total[:, at]
            p = e_scr[slot, :, at] * factor
            p_scr[:, at] = p.astype(BF)
            ds_scr[:, at] = (p * (dp_scr[slot, :, at] - weighted[:, at])).astype(BF)
        dv = jnp.dot(p_scr[...], dos[...], preferred_element_type=F32)
        dk = jnp.dot(ds_scr[...], qs[...], preferred_element_type=F32) * scale
        key_t = kv_block(block, slice(0, hd)).T
        dq_acc[...] += jnp.dot(key_t, ds_scr[...], preferred_element_type=F32)
        chip = lax.div(block, 2)
        mine = lax.rem(block, 2) == core

        @pl.when(mine)
        def _():
            own_out[chip, :, 0:hd] = dk
            own_out[chip, :, hd : 2 * hd] = dv

        @pl.when(jnp.logical_not(mine))
        def _():
            other_out[chip, :, 0:hd] = dk
            other_out[chip, :, hd : 2 * hd] = dv

    for c in range(cols // hd):
        at = slice(c * hd, (c + 1) * hd)
        dq_rows[at, :] = (dq_acc[:, at].T * scale).astype(BF)
    for h in range(HEADS):
        dq_ref[:, h * hd : (h + 1) * hd] = dq_rows[h * rows : (h + 1) * rows, :]


def attention(place, seg_row, own_kv, other_kv, q, do, interpret=False):
    rows, width = q.shape
    hd = width // HEADS
    cols = rows * HEADS
    chips = own_kv.shape[0]
    slots = min(2 * chips, -(-(LONGEST + rows - 1) // rows))
    vmem = pl.BlockSpec(memory_space=pltpu.VMEM)
    return pl.pallas_call(
        attention_kernel,
        out_shape=(
            jax.ShapeDtypeStruct((rows, width), BF),
            jax.ShapeDtypeStruct((chips, rows, 2 * hd), F32),
            jax.ShapeDtypeStruct((chips, rows, 2 * hd), F32),
        ),
        in_specs=[pl.BlockSpec(memory_space=pltpu.SMEM)] + [vmem] * 5,
        out_specs=(vmem, vmem, vmem),
        scratch_shapes=[
            pltpu.VMEM((cols, hd), BF),
            pltpu.VMEM((cols, hd), BF),
            pltpu.VMEM((slots, rows, cols), F32),
            pltpu.VMEM((slots, rows, cols), F32),
            pltpu.VMEM((16, cols), F32),
            pltpu.VMEM((1, cols), F32),
            pltpu.VMEM((1, cols), F32),
            pltpu.VMEM((1, cols), F32),
            pltpu.VMEM((1, cols), F32),
            pltpu.VMEM((rows, cols), BF),
            pltpu.VMEM((rows, cols), BF),
            pltpu.VMEM((hd, cols), F32),
            pltpu.VMEM((cols, hd), BF),
        ],
        compiler_params=pltpu.CompilerParams(vmem_limit_bytes=58 * 1024 * 1024),
        name="attention_backward",
        interpret=interpret,
    )(place, seg_row, own_kv, other_kv, q, do)


def rank_order(core, rank):
    row = lax.broadcasted_iota(jnp.int32, (rank, rank), 0)
    column = lax.broadcasted_iota(jnp.int32, (rank, rank), 1)
    half = rank // 2
    other = (row >= half).astype(jnp.int32)
    spot = row - other * half
    parity = jnp.where(core == 0, other, 1 - other)
    source = (spot // 2) * 4 + parity * 2 + lax.rem(spot, 2)
    return (source == column).astype(BF)


def feature_kernel(place_ref, f_ref, own_ref, other_ref, hi_ref, lo_ref, acc):
    step = pl.program_id(0)
    core = lax.rem(place_ref[0], 2)
    depth = own_ref.shape[0]
    own, other = own_ref[...], other_ref[...]
    even = jnp.where(core == 0, own, other)
    odd = jnp.where(core == 0, other, own)
    part = jnp.dot(f_ref[:, 0:depth], even, preferred_element_type=F32)
    part = part + jnp.dot(f_ref[:, depth : 2 * depth], odd, preferred_element_type=F32)

    @pl.when(step == 0)
    def _():
        acc[...] = part

    @pl.when(step > 0)
    def _():
        acc[...] += part

    @pl.when(step == pl.num_programs(0) - 1)
    def _():
        order = rank_order(core, acc.shape[1])
        whole = acc[...]
        hi = whole.astype(BF)
        lo = (whole - hi.astype(F32)).astype(BF)
        turn = (((1,), (1,)), ((), ()))
        hi_ref[...] = lax.dot_general(order, hi, turn, preferred_element_type=F32).astype(BF)
        lo_ref[...] = lax.dot_general(order, lo, turn, preferred_element_type=F32).astype(BF)


def project_features(place, features, own_p, other_p):
    tok, width = features.shape
    rank = own_p.shape[1]
    depth = own_p.shape[0] // 16
    spec = pl.BlockSpec((depth, rank), lambda i, place: (lax.rem(i, 8) * 2 + i // 8, 0))
    return pl.pallas_call(
        feature_kernel,
        out_shape=(jax.ShapeDtypeStruct((rank, tok), BF), jax.ShapeDtypeStruct((rank, tok), BF)),
        grid_spec=pltpu.PrefetchScalarGridSpec(
            num_scalar_prefetch=1,
            grid=(16,),
            in_specs=[pl.BlockSpec((tok, 2 * depth), lambda i, place: (0, i)), spec, spec],
            out_specs=(
                pl.BlockSpec((rank, tok), lambda i, place: (0, 0)),
                pl.BlockSpec((rank, tok), lambda i, place: (0, 0)),
            ),
            scratch_shapes=[pltpu.VMEM((tok, rank), F32)],
        ),
        name="project_features",
    )(place, features, own_p, other_p)


def outer_kernel(terms_ref, hi_ref, lo_ref, own_ref, other_ref):
    kv = terms_ref[0]
    for i in range(1, terms_ref.shape[0]):
        kv = kv + terms_ref[i]
    kv = kv.astype(BF)
    half = own_ref.shape[0]
    whole = jnp.dot(hi_ref[...], kv, preferred_element_type=F32)
    whole = whole + jnp.dot(lo_ref[...], kv, preferred_element_type=F32)
    own_ref[...] = whole[0:half]
    other_ref[...] = whole[half : 2 * half]


def outer(terms, hi, lo):
    rank, width = hi.shape[0], terms.shape[2]
    return pl.pallas_call(
        outer_kernel,
        out_shape=(
            jax.ShapeDtypeStruct((rank // 2, width), F32),
            jax.ShapeDtypeStruct((rank // 2, width), F32),
        ),
        name="projected_terms",
    )(terms, hi, lo)


def shards(
    queries,
    keys,
    values,
    out_grad,
    segments,
    features,
    projector,
    first_moment,
    second_moment,
    adam_step,
):
    rows = queries.shape[1]
    hd = keys.shape[2]
    ctx = lax.axis_index("ctx")
    core = ctx % 2
    far = lax.axis_index("dp") // 8
    place = ctx.reshape(1).astype(jnp.int32)
    rank = projector.shape[1]

    half = projector.shape[0] // 2
    piece = lax.dynamic_slice_in_dim(projector, core * half, half, 0)
    partner = lax.ppermute(piece, "dp", FAR_PAIRS)
    pair = jnp.where(
        far == 0,
        jnp.concatenate([piece, partner], axis=0),
        jnp.concatenate([partner, piece], axis=0),
    )
    own_p = lax.all_gather(pair, "dp", axis=0, tiled=True, axis_index_groups=Z_RINGS)

    seg = segments[0]
    zeros = jnp.sum((seg == 0).astype(F32))
    ones = jnp.sum((seg == 1).astype(F32))
    notes = jnp.where(lax.broadcasted_iota(jnp.int32, (PAD, 2 * hd), 0) < 8, zeros, ones)
    packed = jnp.concatenate(
        [jnp.concatenate([keys[0], values[0]], axis=1), notes.astype(BF)], axis=0
    )
    chips = 8
    own_kv = lax.all_to_all(
        jnp.broadcast_to(packed[None], (chips,) + packed.shape),
        "ctx",
        0,
        0,
        tiled=True,
        axis_index_groups=SAME_CORE,
    )
    other_kv = lax.ppermute(own_kv, "ctx", CORE_PAIRS)
    seg_row = jnp.tile(seg, HEADS).reshape(1, rows * HEADS)
    dq, own_terms, other_terms = attention(
        place, seg_row, own_kv, other_kv, queries[0], out_grad[0]
    )
    own_p, own_terms, other_terms = lax.optimization_barrier((own_p, own_terms, other_terms))
    other_p = lax.ppermute(own_p, "ctx", CORE_PAIRS)
    terms = own_terms + lax.ppermute(other_terms, "ctx", CORE_PAIRS)
    terms = lax.all_to_all(terms, "ctx", 0, 0, tiled=True, axis_index_groups=SAME_CORE)

    hi, lo = project_features(place, features[0], own_p, other_p)
    own_part, other_part = outer(terms, hi, lo)
    summed = own_part + lax.ppermute(other_part, "ctx", CORE_PAIRS)
    count = 128
    summed = lax.all_to_all(
        summed.reshape(count, 2, 2 * hd),
        ("dp", "ctx"),
        0,
        0,
        tiled=True,
        axis_index_groups=SAME_CORE_ALL,
    )
    projected = jnp.sum(summed, axis=0)
    first_new = BETA_ONE * first_moment + (1.0 - BETA_ONE) * projected
    second_new = BETA_TWO * second_moment + (1.0 - BETA_TWO) * projected * projected
    step_count = adam_step[0].astype(F32)
    bias_first = 1.0 - jnp.power(F32(BETA_ONE), step_count)
    bias_second = 1.0 - jnp.power(F32(BETA_TWO), step_count)
    direction = first_new / bias_first / (jnp.sqrt(second_new / bias_second) + EPSILON)
    own_dir = lax.all_to_all(
        jnp.broadcast_to(direction.astype(BF)[None], (count, 2, 2 * hd)),
        ("dp", "ctx"),
        0,
        0,
        tiled=True,
        axis_index_groups=SAME_CORE_ALL,
    ).reshape(rank // 2, 2 * hd)
    other_dir = lax.ppermute(own_dir, "ctx", CORE_PAIRS)
    slab_rows = projector.shape[0] // 16
    slab = lax.dynamic_slice_in_dim(projector, ctx * slab_rows, slab_rows, 0)
    slab = lax.dot_general(
        slab, rank_order(core, rank), (((1,), (1,)), ((), ())), preferred_element_type=F32
    ).astype(BF)
    update = jnp.dot(slab[:, : rank // 2], own_dir, preferred_element_type=F32)
    update = update + jnp.dot(slab[:, rank // 2 :], other_dir, preferred_element_type=F32)
    return (dq[None], update, first_new, second_new)


def solution(mesh):
    in_specs = (
        P("dp", "ctx", None),
        P("dp", "ctx", None),
        P("dp", "ctx", None),
        P("dp", "ctx", None),
        P("dp", "ctx"),
        P("dp", "ctx", None),
        P("dp", None),
        P(("dp", "ctx"), None),
        P(("dp", "ctx"), None),
        P(),
    )
    out_specs = (
        P("dp", "ctx", None),
        P(("dp", "ctx"), None),
        P(("dp", "ctx"), None),
        P(("dp", "ctx"), None),
    )
    return jax.shard_map(shards, mesh=mesh, in_specs=in_specs, out_specs=out_specs, check_vma=False)
```

```python
import functools
import math

import jax
import jax.numpy as jnp
from jax import lax
from jax.experimental import pallas as pl
from jax.experimental.pallas import tpu as pltpu
from jax.sharding import PartitionSpec as P

HEADS = 8
BETA_ONE = 0.9
BETA_TWO = 0.999
EPSILON = 1e-08
LONGEST = 2688
PAD = 16
CHUNK = 256
BF = jnp.bfloat16
F32 = jnp.float32

CORE_PAIRS = [(i, i ^ 1) for i in range(16)]
SAME_CORE = [list(range(0, 16, 2)), list(range(1, 16, 2))]
FAR_PAIRS = [(i, i ^ 8) for i in range(16)]
Z_RINGS = [list(range(8)), list(range(8, 16))]
SAME_CORE_ALL = [list(range(0, 256, 2)), list(range(1, 256, 2))]


def attention_kernel(
    place_ref,
    seg_ref,
    own_kv,
    other_kv,
    q_ref,
    do_ref,
    dq_ref,
    own_out,
    other_out,
    qs,
    dos,
    e_scr,
    dp_scr,
    tops,
    top,
    total,
    weighted,
    start_scr,
    dq_acc,
    dq_rows,
):
    rows = q_ref.shape[0]
    hd = q_ref.shape[1] // HEADS
    cols = rows * HEADS
    me = place_ref[0]
    core = lax.rem(me, 2)
    scale = 1.0 / math.sqrt(hd)
    scale_two = scale * math.log2(math.e)
    chunks = cols // CHUNK
    for h in range(HEADS):
        qs[h * rows : (h + 1) * rows, :] = q_ref[:, h * hd : (h + 1) * hd]
        dos[h * rows : (h + 1) * rows, :] = do_ref[:, h * hd : (h + 1) * hd]
    own_out[...] = jnp.zeros_like(own_out)
    other_out[...] = jnp.zeros_like(other_out)
    firsts = jnp.zeros((8, 2 * hd), F32)
    seconds = jnp.zeros((8, 2 * hd), F32)
    for chip in range(own_kv.shape[0]):
        for kv_ref in (own_kv, other_kv):
            line = kv_ref[chip, rows : rows + PAD, :].astype(F32)[0:8]
            firsts = firsts + jnp.where(line == 0.0, 1.0, 0.0)
            seconds = seconds + jnp.where(line < 2.0, 1.0, 0.0)
    first = jnp.sum(firsts[0:1, :], axis=1, keepdims=True)
    second = jnp.sum(seconds[0:1, :], axis=1, keepdims=True)
    low = None
    high = None
    for c in range(chunks):
        at = slice(c * CHUNK, (c + 1) * CHUNK)
        seg = seg_ref[:, at]
        start = jnp.where(seg == 0, 0.0, jnp.where(seg == 1, first, second))
        start_scr[:, at] = start
        low = start if low is None else jnp.minimum(low, start)
        high = start if high is None else jnp.maximum(high, start)
    low_block = lax.div(jnp.min(low).astype(jnp.int32), rows)
    high_key = jnp.max(high).astype(jnp.int32)
    top[...] = jnp.full_like(top, -1e29)
    total[...] = jnp.zeros_like(total)
    weighted[...] = jnp.zeros_like(weighted)
    dq_acc[...] = jnp.zeros_like(dq_acc)

    def kv_block(block, lanes):
        chip = lax.div(block, 2)
        mine = lax.rem(block, 2) == core
        return jnp.where(mine, own_kv[chip, 0:rows, lanes], other_kv[chip, 0:rows, lanes])

    def first_pass(block, masked):
        slot = block - low_block
        key = kv_block(block, slice(0, hd))
        value = kv_block(block, slice(hd, 2 * hd))
        for c in range(chunks):
            at = slice(c * CHUNK, (c + 1) * CHUNK)
            s = lax.dot_general(
                key, qs[at, :], (((1,), (1,)), ((), ())), preferred_element_type=F32
            )
            dp = lax.dot_general(
                value, dos[at, :], (((1,), (1,)), ((), ())), preferred_element_type=F32
            )
            s = s * scale_two
            if masked:
                row = lax.broadcasted_iota(jnp.int32, (rows, CHUNK), 0) + block * rows
                column = lax.broadcasted_iota(jnp.int32, (1, CHUNK), 1) + c * CHUNK
                pos = lax.rem(column, rows) + me * rows
                start = start_scr[:, at].astype(jnp.int32)
                s = jnp.where((row <= pos) & (row >= start), s, -1e30)
            old = top[:, at]
            new = jnp.maximum(old, jnp.max(s, axis=0, keepdims=True))
            e = jnp.exp2(s - new)
            factor = jnp.exp2(old - new)
            top[:, at] = new
            tops[pl.ds(slot, 1), at] = new
            total[:, at] = total[:, at] * factor + jnp.sum(e, axis=0, keepdims=True)
            weighted[:, at] = weighted[:, at] * factor + jnp.sum(e * dp, axis=0, keepdims=True)
            e_scr[slot, :, at] = e
            dp_scr[slot, :, at] = dp

    @pl.loop(low_block, me + 1)
    def _(block):
        edge = (block == me) | (block * rows < high_key)

        @pl.when(edge)
        def _():
            first_pass(block, True)

        @pl.when(jnp.logical_not(edge))
        def _():
            first_pass(block, False)

    inverse = 1.0 / total[...]
    total[...] = inverse
    weighted[...] = weighted[...] * inverse

    @pl.loop(low_block, me + 1)
    def _(block):
        slot = block - low_block
        key_t = kv_block(block, slice(0, hd)).T
        dv = dk = None
        for c in range(chunks):
            at = slice(c * CHUNK, (c + 1) * CHUNK)
            factor = jnp.exp2(tops[pl.ds(slot, 1), at] - top[:, at]) * total[:, at]
            p = e_scr[slot, :, at] * factor
            p_low = p.astype(BF)
            ds = (p * (dp_scr[slot, :, at] - weighted[:, at])).astype(BF)
            dv_part = jnp.dot(p_low, dos[at, :], preferred_element_type=F32)
            dk_part = jnp.dot(ds, qs[at, :], preferred_element_type=F32)
            dv = dv_part if c == 0 else dv + dv_part
            dk = dk_part if c == 0 else dk + dk_part
            dq_acc[:, at] += jnp.dot(key_t, ds, preferred_element_type=F32)
        dk = dk * scale
        chip = lax.div(block, 2)
        mine = lax.rem(block, 2) == core

        @pl.when(mine)
        def _():
            own_out[chip, :, 0:hd] = dk
            own_out[chip, :, hd : 2 * hd] = dv

        @pl.when(jnp.logical_not(mine))
        def _():
            other_out[chip, :, 0:hd] = dk
            other_out[chip, :, hd : 2 * hd] = dv

    for c in range(cols // hd):
        at = slice(c * hd, (c + 1) * hd)
        dq_rows[at, :] = (dq_acc[:, at].T * scale).astype(BF)
    for h in range(HEADS):
        dq_ref[:, h * hd : (h + 1) * hd] = dq_rows[h * rows : (h + 1) * rows, :]


def attention(place, seg_row, own_kv, other_kv, q, do, interpret=False):
    rows, width = q.shape
    hd = width // HEADS
    cols = rows * HEADS
    chips = own_kv.shape[0]
    slots = min(2 * chips, -(-(LONGEST + rows - 1) // rows))
    vmem = pl.BlockSpec(memory_space=pltpu.VMEM)
    return pl.pallas_call(
        attention_kernel,
        out_shape=(
            jax.ShapeDtypeStruct((rows, width), BF),
            jax.ShapeDtypeStruct((chips, rows, 2 * hd), F32),
            jax.ShapeDtypeStruct((chips, rows, 2 * hd), F32),
        ),
        in_specs=[pl.BlockSpec(memory_space=pltpu.SMEM)] + [vmem] * 5,
        out_specs=(vmem, vmem, vmem),
        scratch_shapes=[
            pltpu.VMEM((cols, hd), BF),
            pltpu.VMEM((cols, hd), BF),
            pltpu.VMEM((slots, rows, cols), F32),
            pltpu.VMEM((slots, rows, cols), F32),
            pltpu.VMEM((16, cols), F32),
            pltpu.VMEM((1, cols), F32),
            pltpu.VMEM((1, cols), F32),
            pltpu.VMEM((1, cols), F32),
            pltpu.VMEM((1, cols), F32),
            pltpu.VMEM((hd, cols), F32),
            pltpu.VMEM((cols, hd), BF),
        ],
        compiler_params=pltpu.CompilerParams(vmem_limit_bytes=56 * 1024 * 1024),
        name="attention_backward",
        interpret=interpret,
    )(place, seg_row, own_kv, other_kv, q, do)


def rank_order(core, rank):
    row = lax.broadcasted_iota(jnp.int32, (rank, rank), 0)
    column = lax.broadcasted_iota(jnp.int32, (rank, rank), 1)
    half = rank // 2
    other = (row >= half).astype(jnp.int32)
    spot = row - other * half
    parity = jnp.where(core == 0, other, 1 - other)
    source = (spot // 2) * 4 + parity * 2 + lax.rem(spot, 2)
    return (source == column).astype(BF)


def feature_kernel(near_ref, far_ref, near_two, far_two, p_ref, hi_ref, lo_ref, acc):
    step = pl.program_id(0)
    tok = near_ref.shape[0]
    per_step = 2
    depth = near_ref.shape[1] // per_step

    @pl.when(step == 0)
    def _():
        acc[...] = jnp.zeros_like(acc)

    for j, pair in enumerate(((near_ref, far_ref), (near_two, far_two))):
        total = None
        for z in range(per_step):
            for far in range(2):
                rows = slice((z * 2 + far) * depth, (z * 2 + far + 1) * depth)
                term = jnp.dot(
                    pair[far][:, z * depth : (z + 1) * depth],
                    p_ref[rows, :],
                    preferred_element_type=F32,
                )
                total = term if total is None else total + term
        acc[j * tok : (j + 1) * tok, :] += total

    @pl.when(step == pl.num_programs(0) - 1)
    def _():
        half = acc.shape[1]
        row = lax.broadcasted_iota(jnp.int32, (half, half), 0)
        column = lax.broadcasted_iota(jnp.int32, (half, half), 1)
        unit = (row == column).astype(BF)
        turn = (((1,), (1,)), ((), ()))
        for j in range(2):
            whole = acc[j * tok : (j + 1) * tok, :]
            hi = whole.astype(BF)
            lo = (whole - hi.astype(F32)).astype(BF)
            hi_ref[j] = lax.dot_general(unit, hi, turn, preferred_element_type=F32).astype(BF)
            lo_ref[j] = lax.dot_general(unit, lo, turn, preferred_element_type=F32).astype(BF)


def project_features(features, given, own_p):
    tok, width = features.shape
    half = own_p.shape[1]
    steps = 4
    out = jax.ShapeDtypeStruct((2, half, tok), BF)
    out_spec = pl.BlockSpec((2, half, tok), lambda i: (0, 0, 0))
    near = pl.BlockSpec((tok, width // (2 * steps)), lambda i: (0, i))
    far = pl.BlockSpec((tok, width // (2 * steps)), lambda i: (0, i + 4))
    return pl.pallas_call(
        feature_kernel,
        out_shape=(out, out),
        grid=(steps,),
        in_specs=[
            near,
            far,
            near,
            far,
            pl.BlockSpec((own_p.shape[0] // steps, half), lambda i: (i, 0)),
        ],
        out_specs=(out_spec, out_spec),
        scratch_shapes=[pltpu.VMEM((2 * tok, half), F32)],
        compiler_params=pltpu.CompilerParams(vmem_limit_bytes=56 * 1024 * 1024),
        cost_estimate=pl.CostEstimate(
            flops=tok * width * half * 4, bytes_accessed=12 * 1024 * 1024, transcendentals=0
        ),
        name="project_features",
    )(features, features, given, given, own_p)


def outer_kernel(hi_ref, lo_ref, kv_ref, kv_two, out_ref):
    total = None
    for j, rhs in enumerate((kv_ref, kv_two)):
        for lhs in (hi_ref, lo_ref):
            term = jnp.dot(lhs[j], rhs[...], preferred_element_type=F32)
            total = term if total is None else total + term
    out_ref[...] = total


def outer(hi, lo, kv, kv_two):
    return pl.pallas_call(
        outer_kernel,
        out_shape=jax.ShapeDtypeStruct((hi.shape[1], kv.shape[1]), F32),
        name="projected_terms",
    )(hi, lo, kv, kv_two)


def shards(
    queries,
    keys,
    values,
    out_grad,
    segments,
    features,
    projector,
    first_moment,
    second_moment,
    adam_step,
):
    rows = queries.shape[1]
    hd = keys.shape[2]
    ctx = lax.axis_index("ctx")
    core = ctx % 2
    far = lax.axis_index("dp") // 8
    place = ctx.reshape(1).astype(jnp.int32)
    rank = projector.shape[1]

    given = lax.ppermute(features[0], "ctx", CORE_PAIRS)
    order = rank_order(core, rank)
    piece = lax.dot_general(
        projector, order[: rank // 2], (((1,), (1,)), ((), ())), preferred_element_type=F32
    ).astype(BF)
    partner = lax.ppermute(piece, "dp", FAR_PAIRS)
    seg = segments[0]
    seg_line = jnp.pad(seg, (0, 2 * hd - rows), constant_values=3).astype(BF)
    packed = jnp.concatenate(
        [
            jnp.concatenate([keys[0], values[0]], axis=1),
            jnp.broadcast_to(seg_line[None], (PAD, 2 * hd)),
        ],
        axis=0,
    )
    chips = 8
    copies = jnp.broadcast_to(packed[None], (chips,) + packed.shape)
    partner, copies = lax.optimization_barrier((partner, copies))
    pair = jnp.where(
        far == 0,
        jnp.concatenate([piece, partner], axis=0),
        jnp.concatenate([partner, piece], axis=0),
    )
    own_p = lax.all_gather(pair, "dp", axis=0, tiled=True, axis_index_groups=Z_RINGS)
    own_kv = lax.all_to_all(
        copies,
        "ctx",
        0,
        0,
        tiled=True,
        axis_index_groups=SAME_CORE,
    )
    other_kv = lax.ppermute(own_kv, "ctx", CORE_PAIRS)
    seg_row = jnp.tile(seg, HEADS).reshape(1, rows * HEADS)
    dq, own_terms, other_terms = attention(
        place, seg_row, own_kv, other_kv, queries[0], out_grad[0]
    )
    terms = own_terms + lax.ppermute(other_terms, "ctx", CORE_PAIRS)
    own_p, _ = lax.optimization_barrier((own_p, terms))
    hi, lo = project_features(features[0], given, own_p)
    terms = lax.all_to_all(terms, "ctx", 0, 0, tiled=True, axis_index_groups=SAME_CORE)
    terms, hi, lo = lax.optimization_barrier((terms, hi, lo))
    kv = jnp.sum(terms, axis=0).astype(BF)
    summed = outer(hi, lo, kv, lax.ppermute(kv, "ctx", CORE_PAIRS))
    count = 128
    summed = lax.all_to_all(
        summed.reshape(count, 2, 2 * hd),
        ("dp", "ctx"),
        0,
        0,
        tiled=True,
        axis_index_groups=SAME_CORE_ALL,
    )
    projected = jnp.sum(summed, axis=0)
    first_new = BETA_ONE * first_moment + (1.0 - BETA_ONE) * projected
    second_new = BETA_TWO * second_moment + (1.0 - BETA_TWO) * projected * projected
    step_count = adam_step[0].astype(F32)
    bias_first = 1.0 - jnp.power(F32(BETA_ONE), step_count)
    bias_second = 1.0 - jnp.power(F32(BETA_TWO), step_count)
    direction = first_new / bias_first / (jnp.sqrt(second_new / bias_second) + EPSILON)
    own_dir = lax.all_to_all(
        jnp.broadcast_to(direction.astype(BF)[None], (count, 2, 2 * hd)),
        ("dp", "ctx"),
        0,
        0,
        tiled=True,
        axis_index_groups=SAME_CORE_ALL,
    ).reshape(rank // 2, 2 * hd)
    other_dir = lax.ppermute(own_dir, "ctx", CORE_PAIRS)
    slab_rows = projector.shape[0] // 16
    slab = lax.dynamic_slice_in_dim(projector, ctx * slab_rows, slab_rows, 0)
    slab = lax.dot_general(
        slab, order, (((1,), (1,)), ((), ())), preferred_element_type=F32
    ).astype(BF)
    update = jnp.dot(slab[:, : rank // 2], own_dir, preferred_element_type=F32)
    update = update + jnp.dot(slab[:, rank // 2 :], other_dir, preferred_element_type=F32)
    return (dq[None], update, first_new, second_new)


def solution(mesh):
    in_specs = (
        P("dp", "ctx", None),
        P("dp", "ctx", None),
        P("dp", "ctx", None),
        P("dp", "ctx", None),
        P("dp", "ctx"),
        P("dp", "ctx", None),
        P("dp", None),
        P(("dp", "ctx"), None),
        P(("dp", "ctx"), None),
        P(),
    )
    out_specs = (
        P("dp", "ctx", None),
        P(("dp", "ctx"), None),
        P(("dp", "ctx"), None),
        P(("dp", "ctx"), None),
    )
    return jax.shard_map(shards, mesh=mesh, in_specs=in_specs, out_specs=out_specs, check_vma=False)
```
